512 devices in a mesh: region: 64 (over x, z, core), seg: 8 (over y).
Axes of the slice: x: 4, y: 8, z: 8, core: 2. Of those that a mesh axis runs over, the one named last changes fastest.
Arguments:
- image_start: bfloat16 [1024, 64, 128], P('region'), may hold values from 0 to 1
- tiles: bfloat16 [8, 64, 32, 128, 128], P('seg', 'region'), may hold values from -0.088378906 to 0.088378906
- tile_list: int32 [8, 64, 32, 3], P('seg', 'region'), may hold values from 0 to 63, as said below
- recv_map: int32 [8, 64, 64, 2], P('seg', 'region'), may hold values from 0 to 7
- sinogram: bfloat16 [8, 512, 64, 128], P('seg', 'region'), may hold values from -3 to 3
- weights: bfloat16 [8, 512, 64, 128], P('seg', 'region'), may hold values from 0.25 to 1
Outputs:
- image: bfloat16 [1024, 64, 128], P('region')
The draws below stay inside these ranges and needn't reach their ends.
Inputs may be any that keep to these rules, and one draw needn't show every extreme that they name: `tile_list`: column 0 is a region index below 64, column 1 a slot below 2, column 2 a voxel tile below 16; each bound is reached on every device.
All inputs are finite; a program needn't handle non-finite values.
Results may differ from the reference program's by a relative error of at most 0.0036.
Values may be sent and summed in bfloat16 or wider, within the bound.
No kernel may reach another device: no remote copies, remote signals or barrier semaphores. Data moves between devices by JAX's collectives and lax.ppermute only.
A program may use at most 64 MiB of HBM per device.

```python
import math
import jax
import jax.numpy as jnp
from jax import lax

TILE_WIDTH = 128
SLICE_COUNT = 64
VT = 16
RAY_TILES_LOCAL = 8
NT = 32
CAP = 2
ITERS = 2
VOXTILES = 1024
RAYTILES = 512
N_REGION = 64
N_SEG = 8


def draw_tile_list(key, part):
    key = jax.random.fold_in(key, 11)
    key_peer, key_slot, key_col = jax.random.split(key, 3)
    shape = (N_SEG, N_REGION, NT)
    peers = jax.random.randint(key_peer, shape, 0, N_REGION)
    slots = jax.random.randint(key_slot, shape, 0, CAP)
    cols = jax.random.randint(key_col, shape, 0, VT)
    peers = peers.at[:, :, 1].set(N_REGION - 1)
    slots = slots.at[:, :, 0].set(CAP - 1)
    cols = cols.at[:, :, 2].set(VT - 1)
    return jnp.stack([peers, slots, cols], axis=-1).astype(jnp.int32)


def with_ends(values, rng, least, high):
    dims = values.shape
    place = [jax.random.randint(jax.random.fold_in(rng, axis), (), 0, dims[axis]) for axis in range(len(dims))]
    values = values.at[tuple(place)].set(least)
    longest = dims.index(max(dims))
    place[longest] = (place[longest] + 1) % dims[longest]
    return values.at[tuple(place)].set(high)


def block_levels(stream_key, dims, cuts, smallest, largest):
    def one(dim, parts):
        draws = jax.random.uniform(jax.random.fold_in(jax.random.fold_in(stream_key, 6), dim), (parts,), jnp.float32, smallest / len(cuts), largest / len(cuts))
        return jnp.repeat(jnp.exp(draws), dims[dim] // parts).reshape((-1,) + (1,) * (len(dims) - dim - 1))

    gain = one(*cuts[0])
    for cut in cuts[1:]:
        gain = gain * one(*cut)
    return gain


def noise(stream_key, shape, width, bound, pieces=(), kind=jnp.bfloat16):
    array = jax.random.normal(stream_key, shape, jnp.float32) * width
    if len(pieces) > 0:
        array = block_levels(stream_key, shape, pieces, -0.22, 0.18) * array
    return jnp.clip(array, min=-bound, max=bound).astype(kind)


def setup_inputs(seed: int = 0) -> dict:
    key_list = jax.random.split(jax.random.key(seed), 7)
    image_start = jnp.clip(1.0 * jax.random.uniform(key_list[0], (VOXTILES, SLICE_COUNT, TILE_WIDTH), jnp.float32) ** block_levels(key_list[0], (VOXTILES, SLICE_COUNT, TILE_WIDTH), ((0, 64),), -0.2, 0.2), 0.0, 1.0).astype(jnp.bfloat16)
    tiles = noise(key_list[1], (N_SEG, N_REGION, NT, TILE_WIDTH, TILE_WIDTH), (1.0 / ((NT * TILE_WIDTH / RAY_TILES_LOCAL) ** 0.5 + (NT * N_SEG * TILE_WIDTH / VT) ** 0.5)), 0.088378906, ((0, 8), (1, 64)))
    tile_list = draw_tile_list(jax.random.fold_in(key_list[6], 71), 0)
    recv_map = with_ends(jax.random.randint(key_list[3], (N_SEG, N_REGION, N_REGION, CAP), 0, RAY_TILES_LOCAL), jax.random.fold_in(key_list[3], 1), 0, RAY_TILES_LOCAL - 1).astype(jnp.int32)
    sinogram = noise(key_list[4], (N_SEG, RAYTILES, SLICE_COUNT, TILE_WIDTH), 0.5, 3.0, ((0, 8), (1, 64)))
    weights = jnp.clip(jnp.exp(math.log(1.0) - 1.3862944 * jax.random.uniform(key_list[5], (N_SEG, RAYTILES, SLICE_COUNT, TILE_WIDTH), jnp.float32) ** block_levels(key_list[5], (N_SEG, RAYTILES, SLICE_COUNT, TILE_WIDTH), ((0, 8), (1, 64)), -0.2, 0.2)), 0.25, 1.0).astype(jnp.bfloat16)
    return {"image_start": image_start, "tiles": tiles, "tile_list": tile_list, "recv_map": recv_map, "sinogram": sinogram, "weights": weights}


def segment_backprojection(matrix_tiles_shard, tile_lists_shard, received_shard, measured_shard, weights_shard, image_block):
    peers = tile_lists_shard[..., 0]
    slots = tile_lists_shard[..., 1]
    cols = tile_lists_shard[..., 2]
    dest = peers * CAP + slots
    picked = jax.vmap(lambda xr, c: jnp.take(xr, c, axis=0))(image_block, cols)
    part = jnp.einsum('risk,rijk->risj', picked.astype(jnp.float32), matrix_tiles_shard.astype(jnp.float32))
    sent = jax.vmap(lambda p, d: jax.ops.segment_sum(p, d, num_segments=N_REGION * CAP))(part, dest)
    sent = sent.astype(jnp.bfloat16).reshape(N_REGION, N_REGION, CAP, SLICE_COUNT, TILE_WIDTH)
    got = jnp.transpose(sent, (1, 0, 2, 3, 4)).reshape(N_REGION, N_REGION * CAP, SLICE_COUNT, TILE_WIDTH)
    flat_recv = received_shard.reshape(N_REGION, N_REGION * CAP)
    forward_ray_sums = jax.vmap(lambda g, m: jax.ops.segment_sum(g.astype(jnp.float32), m, num_segments=RAY_TILES_LOCAL))(got, flat_recv)
    measured_sinogram = measured_shard.reshape(N_REGION, RAY_TILES_LOCAL, SLICE_COUNT, TILE_WIDTH).astype(jnp.float32)
    statistical_weights = weights_shard.reshape(N_REGION, RAY_TILES_LOCAL, SLICE_COUNT, TILE_WIDTH).astype(jnp.float32)
    residual_rays = (statistical_weights * (measured_sinogram - forward_ray_sums)).astype(jnp.bfloat16)
    reply = jax.vmap(lambda r, m: jnp.take(r, m, axis=0))(residual_rays, flat_recv)
    reply = reply.reshape(N_REGION, N_REGION, CAP, SLICE_COUNT, TILE_WIDTH)
    back = jnp.transpose(reply, (1, 0, 2, 3, 4)).reshape(N_REGION, N_REGION * CAP, SLICE_COUNT, TILE_WIDTH)
    per_tile = jax.vmap(lambda b, d: jnp.take(b, d, axis=0))(back, dest)
    terms = jnp.einsum('risj,rijk->risk', per_tile.astype(jnp.float32), matrix_tiles_shard.astype(jnp.float32))
    return jax.vmap(lambda t, c: jax.ops.segment_sum(t, c, num_segments=VT))(terms, cols)


def reference(image_start, tiles, tile_list, recv_map, sinogram, weights):
    image = image_start.astype(jnp.float32).reshape(N_REGION, VT, SLICE_COUNT, TILE_WIDTH)
    for step in range(ITERS):
        image_block = image.astype(jnp.bfloat16)

        def one_segment(tile_entries):
            matrix_tiles_shard, tile_lists_shard, received_shard, measured_shard, weights_shard = tile_entries
            return segment_backprojection(matrix_tiles_shard, tile_lists_shard, received_shard, measured_shard, weights_shard, image_block)

        grads = lax.map(one_segment, (tiles, tile_list, recv_map, sinogram, weights))
        grad = jnp.sum(grads, axis=0)
        image = jnp.maximum(image + grad, 0.0)
    return image.reshape(VOXTILES, SLICE_COUNT, TILE_WIDTH).astype(jnp.bfloat16)
```

```python
import jax
import jax.numpy as jnp
from jax import lax
from jax.experimental import pallas as pl
from jax.experimental.pallas import tpu as pltpu
from jax.sharding import Mesh, PartitionSpec as P

CAP = 2
ITERS = 2
BF = jnp.bfloat16
F32 = jnp.float32
NEAR = ("x", "zl", "c")
REGION = ("x", "zh", "zl", "c")

VM = pl.BlockSpec(memory_space=pltpu.VMEM)
SM = pl.BlockSpec(memory_space=pltpu.SMEM)
PARAMS = pltpu.CompilerParams(vmem_limit_bytes=40 * 1024 * 1024)


def slot_row(entries, i):
    owner = entries[i, 0]
    near = ((owner >> 4) << 2) | (owner & 3)
    return near * 8 + ((owner >> 2) & 3) * CAP + entries[i, 1]


def project_kernel(entries, image, mat, out, prod, acc):
    n = mat.shape[0]
    for i in range(n):
        prod[i] = lax.dot_general(
            image[entries[i, 2]], mat[i], (((1,), (1,)), ((), ())), preferred_element_type=F32
        )
    out[...] = jnp.zeros_like(out)
    for i in range(n):
        acc[slot_row(entries, i)] = jnp.zeros(acc.shape[1:], F32)
    for i in range(n):
        row = slot_row(entries, i)
        acc[row] = acc[row] + prod[i]
    for i in range(n):
        row = slot_row(entries, i)
        out[row] = acc[row].astype(BF)


def project(entries, image, mat):
    n, slices, width = mat.shape[0], image.shape[1], image.shape[2]
    return pl.pallas_call(
        project_kernel,
        out_shape=jax.ShapeDtypeStruct((128, slices, width), BF),
        in_specs=[SM, VM, VM],
        out_specs=VM,
        scratch_shapes=[pltpu.VMEM((n, slices, width), F32), pltpu.VMEM((128, slices, width), F32)],
        compiler_params=PARAMS,
    )(entries, image, mat)


def near_sum_kernel(far, m0, m1, m2, m3, got, o0, o1, o2, o3, acc):
    maps, outs = (m0, m1, m2, m3), (o0, o1, o2, o3)
    zh = far[0]
    for j in range(4):
        owner = (zh + j) & 3
        m = maps[(4 - j) % 4]
        acc[...] = jnp.zeros_like(acc)
        for near in range(16):
            q = (near >> 2) * 16 + zh * 4 + (near & 3)
            for c in range(CAP):
                t = m[q * CAP + c]
                acc[t] = acc[t] + got[near * 8 + owner * CAP + c].astype(F32)
        outs[j][...] = acc[...].astype(BF)


def near_sum(far, maps, got):
    slices, width = got.shape[1:]
    one = jax.ShapeDtypeStruct((8, slices, width), BF)
    return pl.pallas_call(
        near_sum_kernel,
        out_shape=(one,) * 4,
        in_specs=[SM] * 5 + [VM],
        out_specs=(VM,) * 4,
        scratch_shapes=[pltpu.VMEM((8, slices, width), F32)],
        compiler_params=PARAMS,
    )(far, *maps, got)


def residual_kernel(p0, p1, p2, p3, sino, wts, out):
    total = (p0[...].astype(F32) + p1[...].astype(F32)) + (p2[...].astype(F32) + p3[...].astype(F32))
    out[...] = (wts[...].astype(F32) * (sino[...].astype(F32) - total)).astype(BF)


def residual(parts, sino, wts):
    return pl.pallas_call(
        residual_kernel,
        out_shape=jax.ShapeDtypeStruct(sino.shape, BF),
        in_specs=[VM] * 6,
        out_specs=VM,
        compiler_params=PARAMS,
    )(*parts, sino, wts)


def select_kernel(far, m0, m1, m2, m3, r0, r1, r2, r3, out):
    maps, res = (m0, m1, m2, m3), (r0, r1, r2, r3)
    zh = far[0]
    for j in range(4):
        owner = (zh + 4 - j) & 3
        for near in range(16):
            q = (near >> 2) * 16 + zh * 4 + (near & 3)
            for c in range(CAP):
                out[near * 8 + owner * CAP + c] = res[j][maps[j][q * CAP + c]]


def select(far, maps, res):
    slices, width = res[0].shape[1:]
    return pl.pallas_call(
        select_kernel,
        out_shape=jax.ShapeDtypeStruct((128, slices, width), BF),
        in_specs=[SM] * 5 + [VM] * 4,
        out_specs=VM,
        compiler_params=PARAMS,
    )(far, *maps, *res)


def backproject_kernel(entries, reply, mat, out, prod, acc):
    n = mat.shape[0]
    for i in range(n):
        prod[i] = jnp.dot(reply[slot_row(entries, i)], mat[i], preferred_element_type=F32)
    acc[...] = jnp.zeros_like(acc)
    for i in range(n):
        v = entries[i, 2]
        acc[v] = acc[v] + prod[i]
    out[...] = acc[...].astype(BF)


def backproject(entries, reply, mat, vox_tiles):
    n, slices, width = mat.shape[0], reply.shape[1], reply.shape[2]
    return pl.pallas_call(
        backproject_kernel,
        out_shape=jax.ShapeDtypeStruct((vox_tiles, slices, width), BF),
        in_specs=[SM, VM, VM],
        out_specs=VM,
        scratch_shapes=[pltpu.VMEM((n, slices, width), F32), pltpu.VMEM((vox_tiles, slices, width), F32)],
        compiler_params=PARAMS,
    )(entries, reply, mat)


def update_kernel(got, mine, new, spread):
    own = mine.shape[0]
    segs = got.shape[0] // own
    total = got[0:own].astype(F32)
    for s in range(1, segs):
        total = total + got[s * own : (s + 1) * own].astype(F32)
    x = jnp.maximum(mine[...] + total, 0.0)
    new[...] = x
    rounded = x.astype(BF)
    for s in range(segs):
        spread[s * own : (s + 1) * own] = rounded


def update(got, mine):
    return pl.pallas_call(
        update_kernel,
        out_shape=(jax.ShapeDtypeStruct(mine.shape, F32), jax.ShapeDtypeStruct(got.shape, BF)),
        in_specs=[VM, VM],
        out_specs=(VM, VM),
        compiler_params=PARAMS,
    )(got, mine)


def exchange(v, axes):
    return lax.all_to_all(v, axes, split_axis=0, concat_axis=0, tiled=True)


def far_send(v, j):
    return v if j == 0 else lax.ppermute(v, "zh", [(i, (i + j) % 4) for i in range(4)])


def per_device(image_start, tiles, tile_list, recv_map, sinogram, weights):
    mat = tiles[0, 0]
    entries = tile_list[0, 0]
    flat_map = recv_map[0, 0].reshape(-1)
    sino, wts = sinogram[0], weights[0]
    vox_tiles = image_start.shape[0]
    own = vox_tiles // lax.axis_size("y")
    far = lax.axis_index("zh").astype(jnp.int32).reshape(1)
    maps = [far_send(flat_map, j) for j in range(4)]
    mine = lax.dynamic_slice_in_dim(image_start, lax.axis_index("y") * own, own, 0).astype(F32)
    image = image_start
    for _ in range(ITERS):
        got = exchange(project(entries, image, mat), NEAR)
        sums = near_sum(far, maps, got)
        res = residual([far_send(sums[j], j) for j in range(4)], sino, wts)
        reply = exchange(select(far, maps, [far_send(res, j) for j in range(4)]), NEAR)
        grads = exchange(backproject(entries, reply, mat, vox_tiles), "y")
        mine, spread = update(grads, mine)
        image = exchange(spread, "y")
    return image


def solution(mesh):
    fine = Mesh(mesh.devices.reshape(4, 4, 2, 2, 8), ("x", "zh", "zl", "c", "y"))
    return jax.shard_map(
        per_device,
        mesh=fine,
        in_specs=(
            P(REGION, None, None),
            P("y", REGION, None, None, None),
            P("y", REGION, None, None),
            P("y", REGION, None, None),
            P("y", REGION, None, None),
            P("y", REGION, None, None),
        ),
        out_specs=P(REGION, None, None),
        check_vma=False,
    )
```

```python
import jax
import jax.numpy as jnp
from jax import lax
from jax.experimental import pallas as pl
from jax.experimental.pallas import tpu as pltpu
from jax.sharding import Mesh, PartitionSpec as P

CAP = 2
ITERS = 2
BF = jnp.bfloat16
F32 = jnp.float32
NEAR = ("x", "zl", "c")
REGION = ("x", "zh", "zl", "c")

VM = pl.BlockSpec(memory_space=pltpu.VMEM)
SM = pl.BlockSpec(memory_space=pltpu.SMEM)
PARAMS = pltpu.CompilerParams(vmem_limit_bytes=40 * 1024 * 1024)


def slot_row(entries, i):
    owner = entries[i, 0]
    near = ((owner >> 4) << 2) | (owner & 3)
    return near * 8 + ((owner >> 2) & 3) * CAP + entries[i, 1]


def project_kernel(entries, image, mat, out, prod, acc):
    n = mat.shape[0]
    for i in range(n):
        prod[i] = lax.dot_general(
            image[entries[i, 2]], mat[i], (((1,), (1,)), ((), ())), preferred_element_type=F32
        )
    out[...] = jnp.zeros_like(out)
    for i in range(n):
        acc[slot_row(entries, i)] = jnp.zeros(acc.shape[1:], F32)
    for i in range(n):
        row = slot_row(entries, i)
        acc[row] = acc[row] + prod[i]
    for i in range(n):
        row = slot_row(entries, i)
        out[row] = acc[row].astype(BF)


def project(entries, image, mat):
    n, slices, width = mat.shape[0], image.shape[1], image.shape[2]
    return pl.pallas_call(
        project_kernel,
        out_shape=jax.ShapeDtypeStruct((128, slices, width), BF),
        in_specs=[SM, VM, VM],
        out_specs=VM,
        scratch_shapes=[pltpu.VMEM((n, slices, width), F32), pltpu.VMEM((128, slices, width), F32)],
        compiler_params=PARAMS,
    )(entries, image, mat)


def near_sum_kernel(place, m0, m1, m2, m3, got, out, acc):
    zh = place[0]
    acc[...] = jnp.zeros_like(acc)
    for j, m in enumerate((m0, m1, m2, m3)):
        owner = (zh + 4 - j) & 3
        for near in range(16):
            q = (near >> 2) * 16 + zh * 4 + (near & 3)
            for c in range(CAP):
                t = owner * 8 + m[q * CAP + c]
                acc[t] = acc[t] + got[near * 8 + owner * CAP + c].astype(F32)
    out[...] = acc[...].astype(BF)


def near_sum(place, maps, got):
    slices, width = got.shape[1:]
    return pl.pallas_call(
        near_sum_kernel,
        out_shape=jax.ShapeDtypeStruct((32, slices, width), BF),
        in_specs=[SM] * 5 + [VM],
        out_specs=VM,
        scratch_shapes=[pltpu.VMEM((32, slices, width), F32)],
        compiler_params=PARAMS,
    )(place, *maps, got)


def residual_kernel(parts, sino, wts, out):
    n = sino.shape[0]
    total = parts[0:n].astype(F32)
    for k in range(1, 4):
        total = total + parts[k * n : (k + 1) * n].astype(F32)
    res = (wts[...].astype(F32) * (sino[...].astype(F32) - total)).astype(BF)
    for k in range(4):
        out[k * n : (k + 1) * n] = res


def residual(parts, sino, wts):
    return pl.pallas_call(
        residual_kernel,
        out_shape=jax.ShapeDtypeStruct(parts.shape, BF),
        in_specs=[VM] * 3,
        out_specs=VM,
        compiler_params=PARAMS,
    )(parts, sino, wts)


def select_kernel(place, m0, m1, m2, m3, res, out):
    zh = place[0]
    for j, m in enumerate((m0, m1, m2, m3)):
        owner = (zh + 4 - j) & 3
        for near in range(16):
            q = (near >> 2) * 16 + zh * 4 + (near & 3)
            for c in range(CAP):
                out[near * 8 + owner * CAP + c] = res[owner * 8 + m[q * CAP + c]]


def select(place, maps, res):
    slices, width = res.shape[1:]
    return pl.pallas_call(
        select_kernel,
        out_shape=jax.ShapeDtypeStruct((128, slices, width), BF),
        in_specs=[SM] * 5 + [VM],
        out_specs=VM,
        compiler_params=PARAMS,
    )(place, *maps, res)


def backproject_kernel(entries, reply, mat, out, prod, acc):
    n = mat.shape[0]
    for i in range(n):
        prod[i] = jnp.dot(reply[slot_row(entries, i)], mat[i], preferred_element_type=F32)
    acc[...] = jnp.zeros_like(acc)
    for i in range(n):
        v = entries[i, 2]
        acc[v] = acc[v] + prod[i]
    out[...] = acc[...].astype(BF)


def backproject(entries, reply, mat, vox_tiles):
    n, slices, width = mat.shape[0], reply.shape[1], reply.shape[2]
    return pl.pallas_call(
        backproject_kernel,
        out_shape=jax.ShapeDtypeStruct((vox_tiles, slices, width), BF),
        in_specs=[SM, VM, VM],
        out_specs=VM,
        scratch_shapes=[pltpu.VMEM((n, slices, width), F32), pltpu.VMEM((vox_tiles, slices, width), F32)],
        compiler_params=PARAMS,
    )(entries, reply, mat)


def update_kernel(place, got, mine, new, spread):
    own = new.shape[0]
    segs = got.shape[0] // own
    total = got[0:own].astype(F32)
    for s in range(1, segs):
        total = total + got[s * own : (s + 1) * own].astype(F32)
    at = 0 if mine.shape[0] == own else place[1]
    x = jnp.maximum(mine[pl.ds(at, own)].astype(F32) + total, 0.0)
    new[...] = x
    rounded = x.astype(BF)
    for s in range(segs):
        spread[s * own : (s + 1) * own] = rounded


def update(place, got, mine, own):
    return pl.pallas_call(
        update_kernel,
        out_shape=(
            jax.ShapeDtypeStruct((own,) + got.shape[1:], F32),
            jax.ShapeDtypeStruct(got.shape, BF),
        ),
        in_specs=[SM, VM, VM],
        out_specs=(VM, VM),
        compiler_params=PARAMS,
    )(place, got, mine)


def exchange(v, axes):
    return lax.all_to_all(v, axes, split_axis=0, concat_axis=0, tiled=True)


def far_send(v, j):
    return v if j == 0 else lax.ppermute(v, "zh", [(i, (i + j) % 4) for i in range(4)])


def per_device(image_start, tiles, tile_list, recv_map, sinogram, weights):
    mat = tiles[0, 0]
    entries = tile_list[0, 0]
    flat_map = recv_map[0, 0].reshape(-1)
    sino, wts = sinogram[0], weights[0]
    vox_tiles = image_start.shape[0]
    own = vox_tiles // lax.axis_size("y")
    place = jnp.stack([lax.axis_index("zh"), lax.axis_index("y") * own]).astype(jnp.int32)
    maps = [far_send(flat_map, j) for j in range(4)]
    image = mine = image_start
    for _ in range(ITERS):
        got = exchange(project(entries, image, mat), NEAR)
        parts = exchange(near_sum(place, maps, got), "zh")
        res = exchange(residual(parts, sino, wts), "zh")
        reply = exchange(select(place, maps, res), NEAR)
        grads = exchange(backproject(entries, reply, mat, vox_tiles), "y")
        mine, spread = update(place, grads, mine, own)
        image = exchange(spread, "y")
    return image


def solution(mesh):
    fine = Mesh(mesh.devices.reshape(4, 4, 2, 2, 8), ("x", "zh", "zl", "c", "y"))
    return jax.shard_map(
        per_device,
        mesh=fine,
        in_specs=(
            P(REGION, None, None),
            P("y", REGION, None, None, None),
            P("y", REGION, None, None),
            P("y", REGION, None, None),
            P("y", REGION, None, None),
            P("y", REGION, None, None),
        ),
        out_specs=P(REGION, None, None),
        check_vma=False,
    )
```

```python
import jax
import jax.numpy as jnp
from jax import lax
from jax.experimental import pallas as pl
from jax.experimental.pallas import tpu as pltpu
from jax.sharding import Mesh, PartitionSpec as P

CAP = 2
ITERS = 2
BF = jnp.bfloat16
F32 = jnp.float32
NEAR = ("x", "zl", "c")
REGION = ("x", "zh", "zl", "c")

VM = pl.BlockSpec(memory_space=pltpu.VMEM)
SM = pl.BlockSpec(memory_space=pltpu.SMEM)
BIG = pltpu.CompilerParams(vmem_limit_bytes=56 * 1024 * 1024)
PARAMS = pltpu.CompilerParams(vmem_limit_bytes=40 * 1024 * 1024)


def slot_row(entries, i):
    owner = entries[0, 0, i]
    near = ((owner >> 4) << 2) | (owner & 3)
    return near * 8 + ((owner >> 2) & 3) * CAP + entries[1, 0, i]


def project_tiles(entries, image, mat, out, prod, acc, tiles):
    share = out.shape[0] // mat.shape[0]
    for i in tiles:
        prod[i] = lax.dot_general(
            image[entries[2, 0, i]], mat[i], (((1,), (1,)), ((), ())), preferred_element_type=F32
        )
        out[i * share : (i + 1) * share] = jnp.zeros((share,) + out.shape[1:], BF)
        acc[slot_row(entries, i)] = jnp.zeros(acc.shape[1:], F32)


def sum_slots(entries, out, prod, acc):
    n = prod.shape[0]
    for i in range(n):
        row = slot_row(entries, i)
        acc[row] = acc[row] + prod[i]
    for i in range(n):
        row = slot_row(entries, i)
        out[row] = acc[row].astype(BF)


def project_kernel(entries, image, mat, out, prod, acc):
    project_tiles(entries, image, mat, out, prod, acc, range(mat.shape[0]))
    sum_slots(entries, out, prod, acc)


def first_project_kernel(entries, image_in, mat_in, out, prod, acc, image, mat, sem):
    parts = sem.shape[0] - 1
    size = mat.shape[0] // parts
    loads = [pltpu.make_async_copy(image_in, image, sem.at[parts])]
    for k in range(parts):
        rows = pl.ds(k * size, size)
        loads.append(pltpu.make_async_copy(mat_in.at[rows], mat.at[rows], sem.at[k]))
    for load in loads:
        load.start()
    loads[0].wait()
    for k in range(parts):
        loads[1 + k].wait()
        project_tiles(entries, image, mat, out, prod, acc, range(k * size, (k + 1) * size))
    sum_slots(entries, out, prod, acc)


def project(entries, image, mat, first):
    n, slices, width = mat.shape[0], image.shape[1], image.shape[2]
    scratch = [pltpu.VMEM((n, slices, width), F32), pltpu.VMEM((128, slices, width), F32)]
    if first:
        scratch += [pltpu.VMEM(image.shape, BF), pltpu.VMEM(mat.shape, BF), pltpu.SemaphoreType.DMA((5,))]
    far_spec = pl.BlockSpec(memory_space=pl.ANY)
    return pl.pallas_call(
        first_project_kernel if first else project_kernel,
        out_shape=jax.ShapeDtypeStruct((128, slices, width), BF),
        in_specs=[SM, far_spec, far_spec] if first else [SM, VM, VM],
        out_specs=VM,
        scratch_shapes=scratch,
        compiler_params=BIG if first else PARAMS,
    )(entries, image, mat)


def near_sum_kernel(place, m0, m1, m2, m3, got, out, acc):
    zh = place[0]
    acc[...] = jnp.zeros_like(acc)
    for j, m in enumerate((m0, m1, m2, m3)):
        owner = (zh + 4 - j) & 3
        for near in range(16):
            q = (near >> 2) * 16 + zh * 4 + (near & 3)
            for c in range(CAP):
                t = owner * 8 + m[c, q]
                acc[t] = acc[t] + got[near * 8 + owner * CAP + c].astype(F32)
    out[...] = acc[...].astype(BF)


def near_sum(place, maps, got):
    slices, width = got.shape[1:]
    return pl.pallas_call(
        near_sum_kernel,
        out_shape=jax.ShapeDtypeStruct((32, slices, width), BF),
        in_specs=[SM] * 5 + [VM],
        out_specs=VM,
        scratch_shapes=[pltpu.VMEM((32, slices, width), F32)],
        compiler_params=PARAMS,
    )(place, *maps, got)


def residual_kernel(parts, sino, wts, out):
    n = sino.shape[0]
    total = parts[0:n].astype(F32)
    for k in range(1, 4):
        total = total + parts[k * n : (k + 1) * n].astype(F32)
    out[...] = (wts[...].astype(F32) * (sino[...].astype(F32) - total)).astype(BF)


def residual(parts, sino, wts):
    return pl.pallas_call(
        residual_kernel,
        out_shape=jax.ShapeDtypeStruct(sino.shape, BF),
        in_specs=[VM] * 3,
        out_specs=VM,
        compiler_params=PARAMS,
    )(parts, sino, wts)


def select_kernel(place, m0, m1, m2, m3, res, out):
    zh = place[0]
    for j, m in enumerate((m0, m1, m2, m3)):
        owner = (zh + 4 - j) & 3
        for near in range(16):
            q = (near >> 2) * 16 + zh * 4 + (near & 3)
            for c in range(CAP):
                out[near * 8 + owner * CAP + c] = res[owner * 8 + m[c, q]]


def select(place, maps, res):
    slices, width = res.shape[1:]
    return pl.pallas_call(
        select_kernel,
        out_shape=jax.ShapeDtypeStruct((128, slices, width), BF),
        in_specs=[SM] * 5 + [VM],
        out_specs=VM,
        compiler_params=PARAMS,
    )(place, *maps, res)


def backproject_kernel(entries, reply, mat, out, prod, acc):
    n = mat.shape[0]
    for i in range(n):
        prod[i] = jnp.dot(reply[slot_row(entries, i)], mat[i], preferred_element_type=F32)
    acc[...] = jnp.zeros_like(acc)
    for i in range(n):
        v = entries[2, 0, i]
        acc[v] = acc[v] + prod[i]
    out[...] = acc[...].astype(BF)


def backproject(entries, reply, mat, vox_tiles):
    n, slices, width = mat.shape[0], reply.shape[1], reply.shape[2]
    return pl.pallas_call(
        backproject_kernel,
        out_shape=jax.ShapeDtypeStruct((vox_tiles, slices, width), BF),
        in_specs=[SM, VM, VM],
        out_specs=VM,
        scratch_shapes=[pltpu.VMEM((n, slices, width), F32), pltpu.VMEM((vox_tiles, slices, width), F32)],
        compiler_params=PARAMS,
    )(entries, reply, mat)


def update_kernel(place, got, mine, spread, *new):
    segs = lax.axis_size("y")
    own = got.shape[0] // segs
    total = got[0:own].astype(F32)
    for s in range(1, segs):
        total = total + got[s * own : (s + 1) * own].astype(F32)
    at = 0 if mine.shape[0] == own else place[1]
    x = jnp.maximum(mine[pl.ds(at, own)].astype(F32) + total, 0.0)
    for ref in new:
        ref[...] = x
    rounded = x.astype(BF)
    for s in range(segs):
        spread[s * own : (s + 1) * own] = rounded


def update(place, got, mine, own, last):
    shapes = [jax.ShapeDtypeStruct(got.shape, BF)]
    if not last:
        shapes.append(jax.ShapeDtypeStruct((own,) + got.shape[1:], F32))
    out = pl.pallas_call(
        update_kernel,
        out_shape=shapes,
        in_specs=[SM, VM, VM],
        out_specs=[VM] * len(shapes),
        compiler_params=PARAMS,
    )(place, got, mine)
    return out[0], None if last else out[1]


def exchange(v, axes):
    return lax.all_to_all(v, axes, split_axis=0, concat_axis=0, tiled=True)


def far_send(v, j):
    return v if j == 0 else lax.ppermute(v, "zh", [(i, (i + j) % 4) for i in range(4)])


def per_device(image_start, tiles, tile_list, recv_map, sinogram, weights):
    mat = tiles[0, 0]
    entries = jnp.transpose(tile_list[0], (2, 0, 1))
    own_map = recv_map[0, 0].T
    sino, wts = sinogram[0], weights[0]
    vox_tiles = image_start.shape[0]
    own = vox_tiles // lax.axis_size("y")
    place = jnp.stack([lax.axis_index("zh"), lax.axis_index("y") * own]).astype(jnp.int32)
    maps = [far_send(own_map, j) for j in range(4)]
    image = mine = image_start
    for step in range(ITERS):
        got = exchange(project(entries, image, mat, step == 0), NEAR)
        parts = exchange(near_sum(place, maps, got), "zh")
        res = lax.all_gather(residual(parts, sino, wts), "zh", axis=0, tiled=True)
        reply = exchange(select(place, maps, res), NEAR)
        grads = exchange(backproject(entries, reply, mat, vox_tiles), "y")
        spread, mine = update(place, grads, mine, own, step == ITERS - 1)
        image = exchange(spread, "y")
    return image


def solution(mesh):
    fine = Mesh(mesh.devices.reshape(4, 4, 2, 2, 8), ("x", "zh", "zl", "c", "y"))
    return jax.shard_map(
        per_device,
        mesh=fine,
        in_specs=(
            P(REGION, None, None),
            P("y", REGION, None, None, None),
            P("y", REGION, None, None),
            P("y", REGION, None, None),
            P("y", REGION, None, None),
            P("y", REGION, None, None),
        ),
        out_specs=P(REGION, None, None),
        check_vma=False,
    )
```

```python
import jax
import jax.numpy as jnp
from jax import lax
from jax.experimental import pallas as pl
from jax.experimental.pallas import tpu as pltpu
from jax.sharding import Mesh, PartitionSpec as P

CAP = 2
ITERS = 2
BF = jnp.bfloat16
F32 = jnp.float32
NEAR = ("x", "zl", "c")
REGION = ("x", "zh", "zl", "c")

VM = pl.BlockSpec(memory_space=pltpu.VMEM)
SM = pl.BlockSpec(memory_space=pltpu.SMEM)
BIG = pltpu.CompilerParams(vmem_limit_bytes=56 * 1024 * 1024)
PARAMS = pltpu.CompilerParams(vmem_limit_bytes=40 * 1024 * 1024)


def slot_row(entries, i):
    owner = entries[0, 0, i]
    near = ((owner >> 4) << 2) | (owner & 3)
    return near * 8 + ((owner >> 2) & 3) * CAP + entries[1, 0, i]


def project_tiles(entries, image, mat, out, prod, acc, tiles):
    share = out.shape[0] // mat.shape[0]
    for i in tiles:
        prod[i] = lax.dot_general(
            image[entries[2, 0, i]], mat[i], (((1,), (1,)), ((), ())), preferred_element_type=F32
        )
        out[i * share : (i + 1) * share] = jnp.zeros((share,) + out.shape[1:], BF)
        acc[slot_row(entries, i)] = jnp.zeros(acc.shape[1:], F32)


def sum_slots(entries, out, prod, acc):
    n = prod.shape[0]
    for i in range(n):
        row = slot_row(entries, i)
        acc[row] = acc[row] + prod[i]
    for i in range(n):
        row = slot_row(entries, i)
        out[row] = acc[row].astype(BF)


def project_kernel(entries, image, mat, out, prod, acc):
    project_tiles(entries, image, mat, out, prod, acc, range(mat.shape[0]))
    sum_slots(entries, out, prod, acc)


def first_project_kernel(entries, image_in, mat_in, out, prod, acc, image, mat, rows, blank, last, sem, blank_sem, row_sem):
    parts = sem.shape[0] - 1
    n = mat.shape[0]
    size = n // parts
    loads = [pltpu.make_async_copy(image_in, image, sem.at[parts])]
    for k in range(parts):
        block = pl.ds(k * size, size)
        loads.append(pltpu.make_async_copy(mat_in.at[block], mat.at[block], sem.at[k]))
    for load in loads:
        load.start()
    blank[...] = jnp.zeros_like(blank)
    depth = blank.shape[0]
    blanks = []
    for k in range(out.shape[0] // depth):
        blanks.append(pltpu.make_async_copy(blank, out.at[pl.ds(k * depth, depth)], blank_sem.at[k]))
    for copy in blanks:
        copy.start()
    for i in range(n):
        row = slot_row(entries, i)
        acc[row] = jnp.zeros(acc.shape[1:], F32)
        last[row] = i
    loads[0].wait()
    for k in range(parts):
        loads[1 + k].wait()
        for i in range(k * size, (k + 1) * size):
            prod[i] = lax.dot_general(
                image[entries[2, 0, i]], mat[i], (((1,), (1,)), ((), ())), preferred_element_type=F32
            )
    for i in range(n):
        row = slot_row(entries, i)
        acc[row] = acc[row] + prod[i]
    for copy in blanks:
        copy.wait()
    for i in range(n):
        row = slot_row(entries, i)
        rows[i] = acc[row].astype(BF)

        @pl.when(last[row] == i)
        def _():
            pltpu.make_async_copy(rows.at[i], out.at[row], row_sem.at[i]).start()

    for i in range(n):
        row = slot_row(entries, i)

        @pl.when(last[row] == i)
        def _():
            pltpu.make_async_copy(rows.at[i], out.at[row], row_sem.at[i]).wait()


def project(entries, image, mat, first):
    n, slices, width = mat.shape[0], image.shape[1], image.shape[2]
    scratch = [pltpu.VMEM((n, slices, width), F32), pltpu.VMEM((128, slices, width), F32)]
    if first:
        scratch += [
            pltpu.VMEM(image.shape, BF),
            pltpu.VMEM(mat.shape, BF),
            pltpu.VMEM((n, slices, width), BF),
            pltpu.VMEM((32, slices, width), BF),
            pltpu.SMEM((128,), jnp.int32),
            pltpu.SemaphoreType.DMA((5,)),
            pltpu.SemaphoreType.DMA((4,)),
            pltpu.SemaphoreType.DMA((n,)),
        ]
    loose = pl.BlockSpec(memory_space=pl.ANY)
    return pl.pallas_call(
        first_project_kernel if first else project_kernel,
        out_shape=jax.ShapeDtypeStruct((128, slices, width), BF),
        in_specs=[SM, loose, loose] if first else [SM, VM, VM],
        out_specs=loose if first else VM,
        scratch_shapes=scratch,
        compiler_params=BIG if first else PARAMS,
    )(entries, image, mat)


def near_sum_kernel(place, m0, m1, m2, m3, got, out, a0, a1, a2, a3):
    maps, accs = (m0, m1, m2, m3), (a0, a1, a2, a3)
    zh = place[0]
    owners = [(zh + 4 - j) & 3 for j in range(4)]
    for acc in accs:
        acc[...] = jnp.zeros_like(acc)
    for near in range(16):
        q = (near >> 2) * 16 + zh * 4 + (near & 3)
        for c in range(CAP):
            for owner, m, acc in zip(owners, maps, accs):
                t = m[c, q]
                acc[t] = acc[t] + got[near * 8 + owner * CAP + c].astype(F32)
    for owner, acc in zip(owners, accs):
        out[pl.ds(owner * 8, 8)] = acc[...].astype(BF)


def near_sum(place, maps, got):
    slices, width = got.shape[1:]
    return pl.pallas_call(
        near_sum_kernel,
        out_shape=jax.ShapeDtypeStruct((32, slices, width), BF),
        in_specs=[SM] * 5 + [VM],
        out_specs=VM,
        scratch_shapes=[pltpu.VMEM((8, slices, width), F32)] * 4,
        compiler_params=PARAMS,
    )(place, *maps, got)


def residual_kernel(parts, sino, wts, out):
    n = sino.shape[0]
    total = parts[0:n].astype(F32)
    for k in range(1, 4):
        total = total + parts[k * n : (k + 1) * n].astype(F32)
    out[...] = (wts[...].astype(F32) * (sino[...].astype(F32) - total)).astype(BF)


def residual(parts, sino, wts):
    return pl.pallas_call(
        residual_kernel,
        out_shape=jax.ShapeDtypeStruct(sino.shape, BF),
        in_specs=[VM] * 3,
        out_specs=VM,
        compiler_params=PARAMS,
    )(parts, sino, wts)


def select_kernel(place, m0, m1, m2, m3, res, out):
    zh = place[0]
    for j, m in enumerate((m0, m1, m2, m3)):
        owner = (zh + 4 - j) & 3
        for near in range(16):
            q = (near >> 2) * 16 + zh * 4 + (near & 3)
            for c in range(CAP):
                out[near * 8 + owner * CAP + c] = res[owner * 8 + m[c, q]]


def select(place, maps, res):
    slices, width = res.shape[1:]
    return pl.pallas_call(
        select_kernel,
        out_shape=jax.ShapeDtypeStruct((128, slices, width), BF),
        in_specs=[SM] * 5 + [VM],
        out_specs=VM,
        compiler_params=PARAMS,
    )(place, *maps, res)


def backproject_kernel(entries, reply, mat, out, prod, acc):
    n = mat.shape[0]
    for i in range(n):
        prod[i] = jnp.dot(reply[slot_row(entries, i)], mat[i], preferred_element_type=F32)
    acc[...] = jnp.zeros_like(acc)
    for i in range(n):
        v = entries[2, 0, i]
        acc[v] = acc[v] + prod[i]
    out[...] = acc[...].astype(BF)


def backproject(entries, reply, mat, vox_tiles):
    n, slices, width = mat.shape[0], reply.shape[1], reply.shape[2]
    return pl.pallas_call(
        backproject_kernel,
        out_shape=jax.ShapeDtypeStruct((vox_tiles, slices, width), BF),
        in_specs=[SM, VM, VM],
        out_specs=VM,
        scratch_shapes=[pltpu.VMEM((n, slices, width), F32), pltpu.VMEM((vox_tiles, slices, width), F32)],
        compiler_params=PARAMS,
    )(entries, reply, mat)


def update_kernel(place, got, mine, spread, *new):
    segs = lax.axis_size("y")
    own = got.shape[0] // segs
    total = got[0:own].astype(F32)
    for s in range(1, segs):
        total = total + got[s * own : (s + 1) * own].astype(F32)
    at = 0 if mine.shape[0] == own else place[1]
    x = jnp.maximum(mine[pl.ds(at, own)].astype(F32) + total, 0.0)
    for ref in new:
        ref[...] = x
    rounded = x.astype(BF)
    for s in range(segs):
        spread[s * own : (s + 1) * own] = rounded


def update(place, got, mine, own, last):
    shapes = [jax.ShapeDtypeStruct(got.shape, BF)]
    if not last:
        shapes.append(jax.ShapeDtypeStruct((own,) + got.shape[1:], F32))
    out = pl.pallas_call(
        update_kernel,
        out_shape=shapes,
        in_specs=[SM, VM, VM],
        out_specs=[VM] * len(shapes),
        compiler_params=PARAMS,
    )(place, got, mine)
    return out[0], None if last else out[1]


def exchange(v, axes):
    return lax.all_to_all(v, axes, split_axis=0, concat_axis=0, tiled=True)


def far_send(v, j):
    return v if j == 0 else lax.ppermute(v, "zh", [(i, (i + j) % 4) for i in range(4)])


def per_device(image_start, tiles, tile_list, recv_map, sinogram, weights):
    mat = tiles[0, 0]
    entries = jnp.transpose(tile_list[0], (2, 0, 1))
    own_map = recv_map[0, 0].T
    sino, wts = sinogram[0], weights[0]
    vox_tiles = image_start.shape[0]
    own = vox_tiles // lax.axis_size("y")
    place = jnp.stack([lax.axis_index("zh"), lax.axis_index("y") * own]).astype(jnp.int32)
    maps = [far_send(own_map, j) for j in range(4)]
    image = mine = image_start
    for step in range(ITERS):
        got = exchange(project(entries, image, mat, step == 0), NEAR)
        parts = exchange(near_sum(place, maps, got), "zh")
        res = lax.all_gather(residual(parts, sino, wts), "zh", axis=0, tiled=True)
        reply = exchange(select(place, maps, res), NEAR)
        grads = exchange(backproject(entries, reply, mat, vox_tiles), "y")
        spread, mine = update(place, grads, mine, own, step == ITERS - 1)
        image = exchange(spread, "y")
    return image


def solution(mesh):
    fine = Mesh(mesh.devices.reshape(4, 4, 2, 2, 8), ("x", "zh", "zl", "c", "y"))
    return jax.shard_map(
        per_device,
        mesh=fine,
        in_specs=(
            P(REGION, None, None),
            P("y", REGION, None, None, None),
            P("y", REGION, None, None),
            P("y", REGION, None, None),
            P("y", REGION, None, None),
            P("y", REGION, None, None),
        ),
        out_specs=P(REGION, None, None),
        check_vma=False,
    )
```

```python
import functools

import jax
import jax.numpy as jnp
from jax import lax
from jax.experimental import pallas as pl
from jax.experimental.pallas import tpu as pltpu
from jax.sharding import Mesh, PartitionSpec as P

CAP = 2
ITERS = 2
BF = jnp.bfloat16
F32 = jnp.float32
NEAR = ("x", "zl")
REGION = ("x", "zh", "zl", "c")
ROWS = 256

VM = pl.BlockSpec(memory_space=pltpu.VMEM)
SM = pl.BlockSpec(memory_space=pltpu.SMEM)
PARAMS = pltpu.CompilerParams(vmem_limit_bytes=40 * 1024 * 1024)


def slot_row(entries, a, i):
    owner = entries[0, 0, i]
    near = ((owner >> 4) << 1) | ((owner >> 1) & 1)
    return near * 32 + a * 16 + ((owner >> 2) & 3) * 4 + (owner & 1) * CAP + entries[1, 0, i]


def half(place, slices):
    return pl.ds(pl.multiple_of(place[1] * slices, slices), slices)


def project_kernel(place, e0, e1, *refs):
    images, (m0, m1, out, prod, acc) = refs[:-5], refs[-5:]
    n, slices = m0.shape[0], out.shape[1]
    sides = ((e0, m0, place[1]), (e1, m1, 1 - place[1]))
    for side, (entries, mat, a) in enumerate(sides):
        for i in range(n):
            v = entries[2, 0, i]
            if len(images) == 2:
                x = images[side][v, half(place, slices)]
            else:
                x = images[0][v * 2 + a]
            prod[side * n + i] = lax.dot_general(x, mat[i], (((1,), (1,)), ((), ())), preferred_element_type=F32)
            acc[slot_row(entries, a, i)] = jnp.zeros(acc.shape[1:], F32)
    out[...] = jnp.zeros_like(out)
    for side, (entries, _, a) in enumerate(sides):
        for i in range(n):
            row = slot_row(entries, a, i)
            acc[row] = acc[row] + prod[side * n + i]
    for entries, _, a in sides:
        for i in range(n):
            row = slot_row(entries, a, i)
            out[row] = acc[row].astype(BF)


def project(place, entries, images, mats, slices):
    n, width = mats[0].shape[0], mats[0].shape[2]
    return pl.pallas_call(
        project_kernel,
        out_shape=jax.ShapeDtypeStruct((ROWS, slices, width), BF),
        in_specs=[SM] * 3 + [VM] * (len(images) + 2),
        out_specs=VM,
        scratch_shapes=[pltpu.VMEM((2 * n, slices, width), F32), pltpu.VMEM((ROWS, slices, width), F32)],
        compiler_params=PARAMS,
    )(place, *entries, *images, *mats)


def slot_routes(place, maps):
    zh, c = place[0], place[1]
    for near in range(8):
        for a in range(2):
            q = (near >> 1) * 16 + zh * 4 + (near & 1) * 2 + a
            for s in range(CAP):
                for j, m in enumerate(maps):
                    owner = (zh + 4 - j) & 3
                    for k in range(2):
                        b = c if k == 0 else 1 - c
                        yield near * 32 + a * 16 + owner * 4 + b * CAP + s, j, k, m[k, s, q]


def near_sum_kernel(place, m0, m1, m2, m3, got, out, *accs):
    for acc in accs:
        acc[...] = jnp.zeros_like(acc)
    for row, j, k, t in slot_routes(place, (m0, m1, m2, m3)):
        acc = accs[j * 2 + k]
        acc[t] = acc[t] + got[row].astype(F32)
    for j in range(4):
        for k in range(2):
            b = place[1] if k == 0 else 1 - place[1]
            out[pl.ds(((place[0] + 4 - j) & 3) * 16 + b * 8, 8)] = accs[j * 2 + k][...].astype(BF)


def near_sum(place, maps, got):
    slices, width = got.shape[1:]
    return pl.pallas_call(
        near_sum_kernel,
        out_shape=jax.ShapeDtypeStruct((64, slices, width), BF),
        in_specs=[SM] * 5 + [VM],
        out_specs=VM,
        scratch_shapes=[pltpu.VMEM((8, slices, width), F32)] * 8,
        compiler_params=PARAMS,
    )(place, *maps, got)


def residual_kernel(place, parts, s0, s1, w0, w1, out):
    slices = out.shape[1]
    for k, (sino, wts) in enumerate(((s0, w0), (s1, w1))):
        b = place[1] if k == 0 else 1 - place[1]
        total = parts[pl.ds(b * 8, 8)].astype(F32)
        for z in range(1, 4):
            total = total + parts[pl.ds(z * 16 + b * 8, 8)].astype(F32)
        mine = half(place, slices)
        res = wts[:, mine].astype(F32) * (sino[:, mine].astype(F32) - total)
        out[pl.ds(b * 8, 8)] = res.astype(BF)


def residual(place, parts, sinos, weights):
    return pl.pallas_call(
        residual_kernel,
        out_shape=jax.ShapeDtypeStruct((16,) + parts.shape[1:], BF),
        in_specs=[SM] + [VM] * 5,
        out_specs=VM,
        compiler_params=PARAMS,
    )(place, parts, *sinos, *weights)


def select_kernel(place, m0, m1, m2, m3, res, out):
    for row, j, k, t in slot_routes(place, (m0, m1, m2, m3)):
        b = place[1] if k == 0 else 1 - place[1]
        out[row] = res[((place[0] + 4 - j) & 3) * 16 + b * 8 + t]


def select(place, maps, res):
    slices, width = res.shape[1:]
    return pl.pallas_call(
        select_kernel,
        out_shape=jax.ShapeDtypeStruct((ROWS, slices, width), BF),
        in_specs=[SM] * 5 + [VM],
        out_specs=VM,
        compiler_params=PARAMS,
    )(place, *maps, res)


def backproject_kernel(place, e0, e1, reply, m0, m1, out, prod, acc):
    n = m0.shape[0]
    sides = ((e0, m0, place[1]), (e1, m1, 1 - place[1]))
    for side, (entries, mat, a) in enumerate(sides):
        for i in range(n):
            prod[side * n + i] = jnp.dot(reply[slot_row(entries, a, i)], mat[i], preferred_element_type=F32)
    acc[...] = jnp.zeros_like(acc)
    for side, (entries, _, a) in enumerate(sides):
        for i in range(n):
            v = entries[2, 0, i] * 2 + a
            acc[v] = acc[v] + prod[side * n + i]
    out[...] = acc[...].astype(BF)


def backproject(place, entries, reply, mats, vox_tiles):
    n, slices, width = mats[0].shape[0], reply.shape[1], reply.shape[2]
    return pl.pallas_call(
        backproject_kernel,
        out_shape=jax.ShapeDtypeStruct((2 * vox_tiles, slices, width), BF),
        in_specs=[SM] * 3 + [VM] * 3,
        out_specs=VM,
        scratch_shapes=[pltpu.VMEM((2 * n, slices, width), F32), pltpu.VMEM((2 * vox_tiles, slices, width), F32)],
        compiler_params=PARAMS,
    )(place, *entries, reply, *mats)


def update_kernel(first, last, place, got, *refs):
    olds, outs = refs[: 2 if first else 1], refs[2 if first else 1 :]
    spread = outs[0]
    segs = lax.axis_size("y")
    own, slices = got.shape[0] // segs, got.shape[1]
    total = got[0:own].astype(F32)
    for s in range(1, segs):
        total = total + got[s * own : (s + 1) * own].astype(F32)
    if first:
        state = outs[1]
        for side, old in enumerate(olds):
            a = place[1] if side == 0 else 1 - place[1]
            for k in range(own // 2):
                state[k * 2 + a] = old[place[2] + k, half(place, slices)].astype(F32)
        x = jnp.maximum(state[...] + total, 0.0)
        state[...] = x
    else:
        x = jnp.maximum(olds[0][...] + total, 0.0)
        if not last:
            outs[1][...] = x
    rounded = x.astype(BF)
    for s in range(segs):
        if last:
            for k in range(own):
                spread[s * own + (k % 2) * (own // 2) + k // 2] = rounded[k]
        else:
            spread[s * own : (s + 1) * own] = rounded


def update(place, got, olds, own, last):
    shapes = [jax.ShapeDtypeStruct(got.shape, BF)]
    if not last:
        shapes.append(jax.ShapeDtypeStruct((own,) + got.shape[1:], F32))
    out = pl.pallas_call(
        functools.partial(update_kernel, len(olds) == 2, last),
        out_shape=shapes,
        in_specs=[SM] + [VM] * (1 + len(olds)),
        out_specs=[VM] * len(shapes),
        compiler_params=PARAMS,
    )(place, got, *olds)
    return out[0], out[1:]


def join_kernel(got, out):
    slices = got.shape[1]
    own = got.shape[0] // (2 * lax.axis_size("y"))
    for r in range(got.shape[0]):
        y, c, k = r // (2 * own), r // own % 2, r % own
        out[y * own + k, c * slices : (c + 1) * slices] = got[r]


def join(got, shape):
    return pl.pallas_call(
        join_kernel,
        out_shape=jax.ShapeDtypeStruct(shape, BF),
        in_specs=[VM],
        out_specs=VM,
        compiler_params=PARAMS,
    )(got)


def exchange(v, axes):
    return lax.all_to_all(v, axes, split_axis=0, concat_axis=0, tiled=True)


def far_send(v, j):
    return v if j == 0 else lax.ppermute(v, "zh", [(i, (i + j) % 4) for i in range(4)])


def with_sibling(v):
    return v, lax.ppermute(v, "c", [(0, 1), (1, 0)])


def per_device(image_start, tiles, tile_list, recv_map, sinogram, weights):
    mats = with_sibling(tiles[0, 0])
    images = with_sibling(image_start)
    entries = with_sibling(jnp.transpose(tile_list[0], (2, 0, 1)))
    both_maps = jnp.stack(with_sibling(recv_map[0, 0].T))
    sinos, wts = with_sibling(sinogram[0]), with_sibling(weights[0])
    vox_tiles, slices = image_start.shape[0], image_start.shape[1] // 2
    own = vox_tiles // lax.axis_size("y")
    place = jnp.stack(
        [lax.axis_index("zh"), lax.axis_index("c"), lax.axis_index("y") * own]
    ).astype(jnp.int32)
    maps = [far_send(both_maps, j) for j in range(4)]
    state = images
    for step in range(ITERS):
        last = step == ITERS - 1
        got = exchange(project(place, entries, images, mats, slices), NEAR)
        parts = exchange(near_sum(place, maps, got), "zh")
        res = lax.all_gather(residual(place, parts, sinos, wts), "zh", axis=0, tiled=True)
        reply = exchange(select(place, maps, res), NEAR)
        grads = exchange(backproject(place, entries, reply, mats, vox_tiles), "y")
        spread, state = update(place, grads, state, 2 * own, last)
        images = (exchange(spread, ("y", "c") if last else "y"),)
    return join(images[0], image_start.shape)


def solution(mesh):
    fine = Mesh(mesh.devices.reshape(4, 4, 2, 2, 8), ("x", "zh", "zl", "c", "y"))
    return jax.shard_map(
        per_device,
        mesh=fine,
        in_specs=(
            P(REGION, None, None),
            P("y", REGION, None, None, None),
            P("y", REGION, None, None),
            P("y", REGION, None, None),
            P("y", REGION, None, None),
            P("y", REGION, None, None),
        ),
        out_specs=P(REGION, None, None),
        check_vma=False,
    )
```

```python
import functools

import jax
import jax.numpy as jnp
from jax import lax
from jax.experimental import pallas as pl
from jax.experimental.pallas import tpu as pltpu
from jax.sharding import Mesh, PartitionSpec as P

CAP = 2
ITERS = 2
BF = jnp.bfloat16
F32 = jnp.float32
NEAR = ("x", "zl")
REGION = ("x", "zh", "zl", "c")
ROWS = 256

VM = pl.BlockSpec(memory_space=pltpu.VMEM)
SM = pl.BlockSpec(memory_space=pltpu.SMEM)
BIG = pltpu.CompilerParams(vmem_limit_bytes=58 * 1024 * 1024)
PARAMS = pltpu.CompilerParams(vmem_limit_bytes=40 * 1024 * 1024)


def slot_row(entries, a, i):
    owner = entries[0, 0, i]
    near = ((owner >> 4) << 1) | ((owner >> 1) & 1)
    return near * 32 + a * 16 + ((owner >> 2) & 3) * 4 + (owner & 1) * CAP + entries[1, 0, i]


def half(place, slices):
    return pl.ds(pl.multiple_of(place[1] * slices, slices), slices)


def project_sides(place, sides, image_of, out, prod, acc):
    for side, (entries, mat, a, ready) in enumerate(sides):
        n = mat.shape[0]
        ready()
        for i in range(n):
            x = image_of(side, entries[2, 0, i], a)
            prod[side * n + i] = lax.dot_general(x, mat[i], (((1,), (1,)), ((), ())), preferred_element_type=F32)
            acc[slot_row(entries, a, i)] = jnp.zeros(acc.shape[1:], F32)
    out[...] = jnp.zeros_like(out)
    for side, (entries, mat, a, _) in enumerate(sides):
        for i in range(mat.shape[0]):
            row = slot_row(entries, a, i)
            acc[row] = acc[row] + prod[side * mat.shape[0] + i]
    for entries, mat, a, _ in sides:
        for i in range(mat.shape[0]):
            row = slot_row(entries, a, i)
            out[row] = acc[row].astype(BF)


def project_kernel(place, e0, e1, image, m0, m1, out, prod, acc):
    sides = ((e0, m0, place[1], lambda: None), (e1, m1, 1 - place[1], lambda: None))
    project_sides(place, sides, lambda side, v, a: image[v * 2 + a], out, prod, acc)


def first_project_kernel(place, e0, e1, image_in, image1, mat_in, m1, out, prod, acc, image0, m0, sem):
    slices = out.shape[1]
    loads = [pltpu.make_async_copy(mat_in, m0, sem.at[0]), pltpu.make_async_copy(image_in, image0, sem.at[1])]
    for load in loads:
        load.start()

    def loaded():
        for load in loads:
            load.wait()

    images = (image1, image0)
    sides = ((e1, m1, 1 - place[1], lambda: None), (e0, m0, place[1], loaded))
    project_sides(place, sides, lambda side, v, a: images[side][v, half(place, slices)], out, prod, acc)


def project(place, entries, images, mats, slices):
    n, width = mats[0].shape[0], mats[0].shape[2]
    first = len(images) == 2
    loose = pl.BlockSpec(memory_space=pl.ANY)
    scratch = [pltpu.VMEM((2 * n, slices, width), F32), pltpu.VMEM((ROWS, slices, width), F32)]
    if first:
        scratch += [
            pltpu.VMEM(images[0].shape, BF),
            pltpu.VMEM(mats[0].shape, BF),
            pltpu.SemaphoreType.DMA((2,)),
        ]
    return pl.pallas_call(
        first_project_kernel if first else project_kernel,
        out_shape=jax.ShapeDtypeStruct((ROWS, slices, width), BF),
        in_specs=[SM] * 3 + ([loose, VM, loose, VM] if first else [VM] * 3),
        out_specs=VM,
        scratch_shapes=scratch,
        compiler_params=BIG if first else PARAMS,
    )(place, *entries, *images, *mats)


def slot_routes(place, maps):
    zh, c = place[0], place[1]
    for near in range(8):
        for a in range(2):
            q = (near >> 1) * 16 + zh * 4 + (near & 1) * 2 + a
            for s in range(CAP):
                for j, m in enumerate(maps):
                    owner = (zh + 4 - j) & 3
                    for k in range(2):
                        b = c if k == 0 else 1 - c
                        yield near * 32 + a * 16 + owner * 4 + b * CAP + s, j, k, m[k, s, q]


def near_sum_kernel(place, m0, m1, m2, m3, got, out, *accs):
    for acc in accs:
        acc[...] = jnp.zeros_like(acc)
    for row, j, k, t in slot_routes(place, (m0, m1, m2, m3)):
        acc = accs[j * 2 + k]
        acc[t] = acc[t] + got[row].astype(F32)
    for j in range(4):
        for k in range(2):
            b = place[1] if k == 0 else 1 - place[1]
            out[pl.ds(((place[0] + 4 - j) & 3) * 16 + b * 8, 8)] = accs[j * 2 + k][...].astype(BF)


def near_sum(place, maps, got):
    slices, width = got.shape[1:]
    return pl.pallas_call(
        near_sum_kernel,
        out_shape=jax.ShapeDtypeStruct((64, slices, width), BF),
        in_specs=[SM] * 5 + [VM],
        out_specs=VM,
        scratch_shapes=[pltpu.VMEM((8, slices, width), F32)] * 8,
        compiler_params=PARAMS,
    )(place, *maps, got)


def residual_kernel(place, parts, s0, s1, w0, w1, out):
    slices = out.shape[1]
    for k, (sino, wts) in enumerate(((s0, w0), (s1, w1))):
        b = place[1] if k == 0 else 1 - place[1]
        total = parts[pl.ds(b * 8, 8)].astype(F32)
        for z in range(1, 4):
            total = total + parts[pl.ds(z * 16 + b * 8, 8)].astype(F32)
        mine = half(place, slices)
        res = wts[:, mine].astype(F32) * (sino[:, mine].astype(F32) - total)
        out[pl.ds(b * 8, 8)] = res.astype(BF)


def residual(place, parts, sinos, weights):
    return pl.pallas_call(
        residual_kernel,
        out_shape=jax.ShapeDtypeStruct((16,) + parts.shape[1:], BF),
        in_specs=[SM] + [VM] * 5,
        out_specs=VM,
        compiler_params=PARAMS,
    )(place, parts, *sinos, *weights)


def select_kernel(place, m0, m1, m2, m3, res, out):
    for row, j, k, t in slot_routes(place, (m0, m1, m2, m3)):
        b = place[1] if k == 0 else 1 - place[1]
        out[row] = res[((place[0] + 4 - j) & 3) * 16 + b * 8 + t]


def select(place, maps, res):
    slices, width = res.shape[1:]
    return pl.pallas_call(
        select_kernel,
        out_shape=jax.ShapeDtypeStruct((ROWS, slices, width), BF),
        in_specs=[SM] * 5 + [VM],
        out_specs=VM,
        compiler_params=PARAMS,
    )(place, *maps, res)


def backproject_kernel(place, e0, e1, reply, m0, m1, out, prod, acc):
    n = m0.shape[0]
    sides = ((e0, m0, place[1]), (e1, m1, 1 - place[1]))
    for side, (entries, mat, a) in enumerate(sides):
        for i in range(n):
            prod[side * n + i] = jnp.dot(reply[slot_row(entries, a, i)], mat[i], preferred_element_type=F32)
    acc[...] = jnp.zeros_like(acc)
    for side, (entries, _, a) in enumerate(sides):
        for i in range(n):
            v = entries[2, 0, i] * 2 + a
            acc[v] = acc[v] + prod[side * n + i]
    out[...] = acc[...].astype(BF)


def backproject(place, entries, reply, mats, vox_tiles):
    n, slices, width = mats[0].shape[0], reply.shape[1], reply.shape[2]
    return pl.pallas_call(
        backproject_kernel,
        out_shape=jax.ShapeDtypeStruct((2 * vox_tiles, slices, width), BF),
        in_specs=[SM] * 3 + [VM] * 3,
        out_specs=VM,
        scratch_shapes=[pltpu.VMEM((2 * n, slices, width), F32), pltpu.VMEM((2 * vox_tiles, slices, width), F32)],
        compiler_params=PARAMS,
    )(place, *entries, reply, *mats)


def update_kernel(first, last, place, got, *refs):
    olds, outs = refs[: 2 if first else 1], refs[2 if first else 1 :]
    spread = outs[0]
    segs = lax.axis_size("y")
    own, slices = got.shape[0] // segs, got.shape[1]
    total = got[0:own].astype(F32)
    for s in range(1, segs):
        total = total + got[s * own : (s + 1) * own].astype(F32)
    if first:
        state = outs[1]
        for side, old in enumerate(olds):
            a = place[1] if side == 0 else 1 - place[1]
            for k in range(own // 2):
                state[k * 2 + a] = old[place[2] + k, half(place, slices)].astype(F32)
        x = jnp.maximum(state[...] + total, 0.0)
        state[...] = x
    else:
        x = jnp.maximum(olds[0][...] + total, 0.0)
        if not last:
            outs[1][...] = x
    rounded = x.astype(BF)
    for s in range(segs):
        if last:
            for k in range(own):
                spread[s * own + (k % 2) * (own // 2) + k // 2] = rounded[k]
        else:
            spread[s * own : (s + 1) * own] = rounded


def update(place, got, olds, own, last):
    shapes = [jax.ShapeDtypeStruct(got.shape, BF)]
    if not last:
        shapes.append(jax.ShapeDtypeStruct((own,) + got.shape[1:], F32))
    out = pl.pallas_call(
        functools.partial(update_kernel, len(olds) == 2, last),
        out_shape=shapes,
        in_specs=[SM] + [VM] * (1 + len(olds)),
        out_specs=[VM] * len(shapes),
        compiler_params=PARAMS,
    )(place, got, *olds)
    return out[0], out[1:]


def join_kernel(got, out):
    slices = got.shape[1]
    own = got.shape[0] // (2 * lax.axis_size("y"))
    for r in range(got.shape[0]):
        y, c, k = r // (2 * own), r // own % 2, r % own
        out[y * own + k, c * slices : (c + 1) * slices] = got[r]


def join(got, shape):
    return pl.pallas_call(
        join_kernel,
        out_shape=jax.ShapeDtypeStruct(shape, BF),
        in_specs=[VM],
        out_specs=VM,
        compiler_params=PARAMS,
    )(got)


def exchange(v, axes):
    return lax.all_to_all(v, axes, split_axis=0, concat_axis=0, tiled=True)


def far_send(v, j):
    return v if j == 0 else lax.ppermute(v, "zh", [(i, (i + j) % 4) for i in range(4)])


def with_sibling(v):
    return v, lax.ppermute(v, "c", [(0, 1), (1, 0)])


def per_device(image_start, tiles, tile_list, recv_map, sinogram, weights):
    mats = with_sibling(tiles[0, 0])
    images = with_sibling(image_start)
    entries = with_sibling(jnp.transpose(tile_list[0], (2, 0, 1)))
    both_maps = jnp.stack(with_sibling(recv_map[0, 0].T))
    sinos, wts = with_sibling(sinogram[0]), with_sibling(weights[0])
    vox_tiles, slices = image_start.shape[0], image_start.shape[1] // 2
    own = vox_tiles // lax.axis_size("y")
    place = jnp.stack(
        [lax.axis_index("zh"), lax.axis_index("c"), lax.axis_index("y") * own]
    ).astype(jnp.int32)
    both_maps, sinos, wts = lax.optimization_barrier((both_maps, sinos, wts))
    maps = [far_send(both_maps, j) for j in range(4)]
    state = images
    for step in range(ITERS):
        last = step == ITERS - 1
        got = exchange(project(place, entries, images, mats, slices), NEAR)
        parts = exchange(near_sum(place, maps, got), "zh")
        res = lax.all_gather(residual(place, parts, sinos, wts), "zh", axis=0, tiled=True)
        reply = exchange(select(place, maps, res), NEAR)
        grads = exchange(backproject(place, entries, reply, mats, vox_tiles), "y")
        spread, state = update(place, grads, state, 2 * own, last)
        images = (exchange(spread, ("y", "c") if last else "y"),)
    return join(images[0], image_start.shape)


def solution(mesh):
    fine = Mesh(mesh.devices.reshape(4, 4, 2, 2, 8), ("x", "zh", "zl", "c", "y"))
    return jax.shard_map(
        per_device,
        mesh=fine,
        in_specs=(
            P(REGION, None, None),
            P("y", REGION, None, None, None),
            P("y", REGION, None, None),
            P("y", REGION, None, None),
            P("y", REGION, None, None),
            P("y", REGION, None, None),
        ),
        out_specs=P(REGION, None, None),
        check_vma=False,
    )
```

```python
import functools

import jax
import jax.numpy as jnp
from jax import lax
from jax.experimental import pallas as pl
from jax.experimental.pallas import tpu as pltpu
from jax.sharding import Mesh, PartitionSpec as P

CAP = 2
ITERS = 2
BF = jnp.bfloat16
F32 = jnp.float32
NEAR = ("x", "zl")
REGION = ("x", "zh", "zl", "c")
ROWS = 256

VM = pl.BlockSpec(memory_space=pltpu.VMEM)
SM = pl.BlockSpec(memory_space=pltpu.SMEM)
BIG = pltpu.CompilerParams(vmem_limit_bytes=58 * 1024 * 1024)
PARAMS = pltpu.CompilerParams(vmem_limit_bytes=40 * 1024 * 1024)


def slot_row(entries, a, i):
    owner = entries[0, 0, i]
    near = ((owner >> 4) << 1) | ((owner >> 1) & 1)
    return near * 32 + a * 16 + ((owner >> 2) & 3) * 4 + (owner & 1) * CAP + entries[1, 0, i]


def half(place, slices):
    return pl.ds(pl.multiple_of(place[1] * slices, slices), slices)


def project_sides(place, sides, image_of, out, prod, accs):
    for side, (entries, mat, a, ready) in enumerate(sides):
        n = mat.shape[0]
        ready()
        for i in range(n):
            x = image_of(side, entries[2, 0, i], a)
            prod[side * n + i] = lax.dot_general(x, mat[i], (((1,), (1,)), ((), ())), preferred_element_type=F32)
            accs[side][slot_row(entries, a, i)] = jnp.zeros(accs[side].shape[1:], F32)
    out[...] = jnp.zeros_like(out)
    n = prod.shape[0] // 2
    for i in range(n):
        for side, (entries, _, a, _) in enumerate(sides):
            acc, row = accs[side], slot_row(entries, a, i)
            acc[row] = acc[row] + prod[side * n + i]
    for i in range(n):
        for side, (entries, _, a, _) in enumerate(sides):
            row = slot_row(entries, a, i)
            out[row] = accs[side][row].astype(BF)


def project_kernel(place, e0, e1, image, m0, m1, out, prod, *accs):
    sides = ((e0, m0, place[1], lambda: None), (e1, m1, 1 - place[1], lambda: None))
    project_sides(place, sides, lambda side, v, a: image[v * 2 + a], out, prod, accs)


def first_project_kernel(place, e0, e1, image_in, image1, mat_in, m1, out, prod, acc0, acc1, image0, m0, sem):
    slices = out.shape[1]
    loads = [pltpu.make_async_copy(mat_in, m0, sem.at[0]), pltpu.make_async_copy(image_in, image0, sem.at[1])]
    for load in loads:
        load.start()

    def loaded():
        for load in loads:
            load.wait()

    images = (image1, image0)
    sides = ((e1, m1, 1 - place[1], lambda: None), (e0, m0, place[1], loaded))
    project_sides(place, sides, lambda side, v, a: images[side][v, half(place, slices)], out, prod, (acc0, acc1))


def project(place, entries, images, mats, slices):
    n, width = mats[0].shape[0], mats[0].shape[2]
    first = len(images) == 2
    loose = pl.BlockSpec(memory_space=pl.ANY)
    scratch = [pltpu.VMEM((2 * n, slices, width), F32)] + [pltpu.VMEM((ROWS, slices, width), F32)] * 2
    if first:
        scratch += [
            pltpu.VMEM(images[0].shape, BF),
            pltpu.VMEM(mats[0].shape, BF),
            pltpu.SemaphoreType.DMA((2,)),
        ]
    return pl.pallas_call(
        first_project_kernel if first else project_kernel,
        out_shape=jax.ShapeDtypeStruct((ROWS, slices, width), BF),
        in_specs=[SM] * 3 + ([loose, VM, loose, VM] if first else [VM] * 3),
        out_specs=VM,
        scratch_shapes=scratch,
        compiler_params=BIG if first else PARAMS,
    )(place, *entries, *images, *mats)


def slot_routes(place, maps):
    zh, c = place[0], place[1]
    for near in range(8):
        for a in range(2):
            q = (near >> 1) * 16 + zh * 4 + (near & 1) * 2 + a
            for s in range(CAP):
                for j, m in enumerate(maps):
                    owner = (zh + 4 - j) & 3
                    for k in range(2):
                        b = c if k == 0 else 1 - c
                        yield near * 32 + a * 16 + owner * 4 + b * CAP + s, j, k, m[k, s, q]


def near_sum_kernel(place, m0, m1, m2, m3, got, out, *accs):
    for acc in accs:
        acc[...] = jnp.zeros_like(acc)
    for row, j, k, t in slot_routes(place, (m0, m1, m2, m3)):
        acc = accs[j * 2 + k]
        acc[t] = acc[t] + got[row].astype(F32)
    for j in range(4):
        for k in range(2):
            b = place[1] if k == 0 else 1 - place[1]
            out[pl.ds(((place[0] + 4 - j) & 3) * 16 + b * 8, 8)] = accs[j * 2 + k][...].astype(BF)


def near_sum(place, maps, got):
    slices, width = got.shape[1:]
    return pl.pallas_call(
        near_sum_kernel,
        out_shape=jax.ShapeDtypeStruct((64, slices, width), BF),
        in_specs=[SM] * 5 + [VM],
        out_specs=VM,
        scratch_shapes=[pltpu.VMEM((8, slices, width), F32)] * 8,
        compiler_params=PARAMS,
    )(place, *maps, got)


def residual_kernel(place, parts, s0, s1, w0, w1, out):
    slices = out.shape[1]
    for k, (sino, wts) in enumerate(((s0, w0), (s1, w1))):
        b = place[1] if k == 0 else 1 - place[1]
        total = parts[pl.ds(b * 8, 8)].astype(F32)
        for z in range(1, 4):
            total = total + parts[pl.ds(z * 16 + b * 8, 8)].astype(F32)
        mine = half(place, slices)
        res = wts[:, mine].astype(F32) * (sino[:, mine].astype(F32) - total)
        out[pl.ds(b * 8, 8)] = res.astype(BF)


def residual(place, parts, sinos, weights):
    return pl.pallas_call(
        residual_kernel,
        out_shape=jax.ShapeDtypeStruct((16,) + parts.shape[1:], BF),
        in_specs=[SM] + [VM] * 5,
        out_specs=VM,
        compiler_params=PARAMS,
    )(place, parts, *sinos, *weights)


def select_kernel(place, m0, m1, m2, m3, res, out):
    for row, j, k, t in slot_routes(place, (m0, m1, m2, m3)):
        b = place[1] if k == 0 else 1 - place[1]
        out[row] = res[((place[0] + 4 - j) & 3) * 16 + b * 8 + t]


def select(place, maps, res):
    slices, width = res.shape[1:]
    return pl.pallas_call(
        select_kernel,
        out_shape=jax.ShapeDtypeStruct((ROWS, slices, width), BF),
        in_specs=[SM] * 5 + [VM],
        out_specs=VM,
        compiler_params=PARAMS,
    )(place, *maps, res)


def backproject_kernel(place, e0, e1, reply, m0, m1, out, prod, *accs):
    n = m0.shape[0]
    sides = ((e0, m0, place[1]), (e1, m1, 1 - place[1]))
    for side, (entries, mat, a) in enumerate(sides):
        for i in range(n):
            prod[side * n + i] = jnp.dot(reply[slot_row(entries, a, i)], mat[i], preferred_element_type=F32)
    for acc in accs:
        acc[...] = jnp.zeros_like(acc)
    for i in range(n):
        for side, (entries, _, _) in enumerate(sides):
            acc, v = accs[side], entries[2, 0, i]
            acc[v] = acc[v] + prod[side * n + i]
    for side, (_, _, a) in enumerate(sides):
        for v in range(accs[side].shape[0]):
            out[v * 2 + a] = accs[side][v].astype(BF)


def backproject(place, entries, reply, mats, vox_tiles):
    n, slices, width = mats[0].shape[0], reply.shape[1], reply.shape[2]
    return pl.pallas_call(
        backproject_kernel,
        out_shape=jax.ShapeDtypeStruct((2 * vox_tiles, slices, width), BF),
        in_specs=[SM] * 3 + [VM] * 3,
        out_specs=VM,
        scratch_shapes=[pltpu.VMEM((2 * n, slices, width), F32)] + [pltpu.VMEM((vox_tiles, slices, width), F32)] * 2,
        compiler_params=PARAMS,
    )(place, *entries, reply, *mats)


def update_kernel(first, last, place, got, *refs):
    olds, outs = refs[: 2 if first else 1], refs[2 if first else 1 :]
    spread = outs[0]
    segs = lax.axis_size("y")
    own, slices = got.shape[0] // segs, got.shape[1]
    total = got[0:own].astype(F32)
    for s in range(1, segs):
        total = total + got[s * own : (s + 1) * own].astype(F32)
    if first:
        state = outs[1]
        for side, old in enumerate(olds):
            a = place[1] if side == 0 else 1 - place[1]
            for k in range(own // 2):
                state[k * 2 + a] = old[place[2] + k, half(place, slices)].astype(F32)
        x = jnp.maximum(state[...] + total, 0.0)
        state[...] = x
    else:
        x = jnp.maximum(olds[0][...] + total, 0.0)
        if not last:
            outs[1][...] = x
    rounded = x.astype(BF)
    for s in range(segs):
        if last:
            for k in range(own):
                spread[s * own + (k % 2) * (own // 2) + k // 2] = rounded[k]
        else:
            spread[s * own : (s + 1) * own] = rounded


def update(place, got, olds, own, last):
    shapes = [jax.ShapeDtypeStruct(got.shape, BF)]
    if not last:
        shapes.append(jax.ShapeDtypeStruct((own,) + got.shape[1:], F32))
    out = pl.pallas_call(
        functools.partial(update_kernel, len(olds) == 2, last),
        out_shape=shapes,
        in_specs=[SM] + [VM] * (1 + len(olds)),
        out_specs=[VM] * len(shapes),
        compiler_params=PARAMS,
    )(place, got, *olds)
    return out[0], out[1:]


def join_kernel(got, out):
    slices = got.shape[1]
    own = got.shape[0] // (2 * lax.axis_size("y"))
    for r in range(got.shape[0]):
        y, c, k = r // (2 * own), r // own % 2, r % own
        out[y * own + k, c * slices : (c + 1) * slices] = got[r]


def join(got, shape):
    return pl.pallas_call(
        join_kernel,
        out_shape=jax.ShapeDtypeStruct(shape, BF),
        in_specs=[VM],
        out_specs=VM,
        compiler_params=PARAMS,
    )(got)


def exchange(v, axes):
    return lax.all_to_all(v, axes, split_axis=0, concat_axis=0, tiled=True)


def far_send(v, j):
    return v if j == 0 else lax.ppermute(v, "zh", [(i, (i + j) % 4) for i in range(4)])


def with_sibling(v):
    return v, lax.ppermute(v, "c", [(0, 1), (1, 0)])


def per_device(image_start, tiles, tile_list, recv_map, sinogram, weights):
    mats = with_sibling(tiles[0, 0])
    images = with_sibling(image_start)
    entries = with_sibling(jnp.transpose(tile_list[0], (2, 0, 1)))
    both_maps = jnp.stack(with_sibling(recv_map[0, 0].T))
    sinos, wts = with_sibling(sinogram[0]), with_sibling(weights[0])
    vox_tiles, slices = image_start.shape[0], image_start.shape[1] // 2
    own = vox_tiles // lax.axis_size("y")
    place = jnp.stack(
        [lax.axis_index("zh"), lax.axis_index("c"), lax.axis_index("y") * own]
    ).astype(jnp.int32)
    both_maps, sinos, wts = lax.optimization_barrier((both_maps, sinos, wts))
    maps = [far_send(both_maps, j) for j in range(4)]
    state = images
    for step in range(ITERS):
        last = step == ITERS - 1
        got = exchange(project(place, entries, images, mats, slices), NEAR)
        parts = exchange(near_sum(place, maps, got), "zh")
        res = lax.all_gather(residual(place, parts, sinos, wts), "zh", axis=0, tiled=True)
        reply = exchange(select(place, maps, res), NEAR)
        grads = exchange(backproject(place, entries, reply, mats, vox_tiles), "y")
        spread, state = update(place, grads, state, 2 * own, last)
        images = (exchange(spread, ("y", "c") if last else "y"),)
    return join(images[0], image_start.shape)


def solution(mesh):
    fine = Mesh(mesh.devices.reshape(4, 4, 2, 2, 8), ("x", "zh", "zl", "c", "y"))
    return jax.shard_map(
        per_device,
        mesh=fine,
        in_specs=(
            P(REGION, None, None),
            P("y", REGION, None, None, None),
            P("y", REGION, None, None),
            P("y", REGION, None, None),
            P("y", REGION, None, None),
            P("y", REGION, None, None),
        ),
        out_specs=P(REGION, None, None),
        check_vma=False,
    )
```
